512 devices in a mesh: wide: 64 (over z, x, y_lo), narrow: 8 (over y_hi, core).
Axes of the slice: x: 4, y: 8 (y_hi: 4, y_lo: 2; y = y_hi * 2 + y_lo), z: 8, core: 2. Of those that a mesh axis runs over, the one named last changes fastest.
Arguments:
- output_gradient: bfloat16 [1024, 16384], P('wide', 'narrow'), may hold values from -6 to 6
- packed_weight_codes: int32 [49152, 8192], P('wide', 'narrow'), may hold values from 0 to 255
- group_zero_offsets: int32 [384, 16384], P('wide', 'narrow'), may hold values from 0 to 15
- group_scale_table: float32 [384, 16384], P('wide', 'narrow'), may hold values from 0.0004 to 0.004
- channel_aware_scale: float32 [49152], P('wide'), may hold values from 0.5 to 2
- adapter_down_matrix: bfloat16 [49152, 16], P('wide'), may hold values from -1.5 to 1.5
- adapter_up_matrix: bfloat16 [16, 16384], P(None, 'narrow'), may hold values from -0.046875 to 0.046875
Outputs:
- grad_input: bfloat16 [1024, 49152], P('narrow', 'wide')
The draws below stay inside these ranges and needn't reach their ends.
Inputs may be any that keep to these rules, and one draw needn't show every extreme that they name: `packed_weight_codes`: word column 128 * b + i holds the code of output column 2 * 128 * b + i in its value modulo 16 and that of column 2 * 128 * b + 128 + i in its value divided by 16.
All inputs are finite; a program needn't handle non-finite values.
Results may differ from the reference program's by a relative error of at most 0.0048.
Values may be sent and summed in bfloat16 or wider, within the bound.
No kernel may reach another device: no remote copies, remote signals or barrier semaphores. Data moves between devices by JAX's collectives and lax.ppermute only.
A program may use at most 128 MiB of HBM per device.

```python
import math
import jax
import jax.numpy as jnp
from jax import lax

MODEL_WIDTH = 16384
INPUT_CHANNELS = 49152
GROUP = 128
HALF = 128
ADAPTER_RANK = 16
TOKENS = 1024


def touch_ends(values, own_key, least, top_value):
    shape = values.shape
    place = [jax.random.randint(jax.random.fold_in(own_key, axis), (), 0, shape[axis]) for axis in range(len(shape))]
    values = values.at[tuple(place)].set(least)
    longest = shape.index(max(shape))
    place[longest] = (place[longest] + 1) % shape[longest]
    return values.at[tuple(place)].set(top_value)


def block_levels(stream_key, shape, cuts, smallest, high):
    level = 1.0
    for axis_at, blocks in cuts:
        heights = jax.random.uniform(jax.random.fold_in(jax.random.fold_in(stream_key, 6), axis_at), (blocks,), jnp.float32, smallest / len(cuts), high / len(cuts))
        level = level * jnp.repeat(jnp.exp(heights), shape[axis_at] // blocks).reshape((-1,) + (1,) * (len(shape) - 1 - axis_at))
    return level


def scatter_about(stream_key, dims, width, most, shards=(), held_as=jnp.bfloat16):
    entries = jax.random.normal(stream_key, dims, jnp.float32) * width
    if len(shards) > 0:
        entries = block_levels(stream_key, dims, shards, -0.22, 0.18) * entries
    return jnp.clip(entries, min=-most, max=most).astype(held_as)


def setup_inputs(seed: int = 0) -> dict:
    seeds = jax.random.split(jax.random.key(seed), 8)
    output_gradient = scatter_about(seeds[0], (TOKENS, MODEL_WIDTH), 1.0, 6.0, ((0, 64), (1, 8)))
    packed_weight_codes = touch_ends(jax.random.randint(seeds[1], (INPUT_CHANNELS, MODEL_WIDTH // 2), 0, 256), jax.random.fold_in(seeds[1], 1), 0, 255).astype(jnp.int32)
    group_zero_offsets = touch_ends(jax.random.randint(seeds[2], (INPUT_CHANNELS // GROUP, MODEL_WIDTH), 0, 16), jax.random.fold_in(seeds[2], 1), 0, 15).astype(jnp.int32)
    group_scale_table = jnp.clip(jnp.exp(math.log(0.004) - 2.3025852 * jax.random.uniform(seeds[3], (INPUT_CHANNELS // GROUP, MODEL_WIDTH), jnp.float32) ** block_levels(seeds[3], (INPUT_CHANNELS // GROUP, MODEL_WIDTH), ((0, 64), (1, 8)), -0.2, 0.2)), 0.0004, 0.004)
    channel_aware_scale = jnp.clip(jnp.exp(math.log(2.0) - 1.3862944 * jax.random.uniform(seeds[4], (INPUT_CHANNELS,), jnp.float32) ** block_levels(seeds[4], (INPUT_CHANNELS,), ((0, 64),), -0.2, 0.2)), 0.5, 2.0)
    adapter_down_matrix = scatter_about(seeds[5], (INPUT_CHANNELS, ADAPTER_RANK), ADAPTER_RANK ** -0.5, 1.5, ((0, 64),))
    adapter_up_matrix = scatter_about(seeds[6], (ADAPTER_RANK, MODEL_WIDTH), MODEL_WIDTH ** -0.5, 0.046875, ((1, 8),))
    return dict(output_gradient=output_gradient, packed_weight_codes=packed_weight_codes, group_zero_offsets=group_zero_offsets, group_scale_table=group_scale_table, channel_aware_scale=channel_aware_scale, adapter_down_matrix=adapter_down_matrix, adapter_up_matrix=adapter_up_matrix)


adapter_gain = 0.5


def unpack(words, zero_rows, scale_rows):
    rows, half_cols = words.shape
    low_codes = words % 16
    high_codes = words // 16
    blocks = half_cols // HALF
    codes = jnp.stack([low_codes.reshape(rows, blocks, HALF), high_codes.reshape(rows, blocks, HALF)], axis=2).reshape(rows, 2 * half_cols)
    groups = rows // GROUP
    shifted = (codes.reshape(groups, GROUP, 2 * half_cols) - zero_rows[:, None, :]).astype(jnp.float32)
    return (shifted * scale_rows[:, None, :]).reshape(rows, 2 * half_cols).astype(jnp.bfloat16)


def reference(output_gradient, packed_weight_codes, group_zero_offsets, group_scale_table, channel_aware_scale, adapter_down_matrix, adapter_up_matrix):
    block = GROUP * 8
    grad_float = output_gradient.astype(jnp.float32)

    def one_block(index):
        start = (index * block).astype(jnp.int32)
        first_group = (index * 8).astype(jnp.int32)
        words = lax.dynamic_slice_in_dim(packed_weight_codes, start, block, 0)
        zero_rows = lax.dynamic_slice_in_dim(group_zero_offsets, first_group, 8, 0)
        scale_rows = lax.dynamic_slice_in_dim(group_scale_table, first_group, 8, 0)
        weight = unpack(words, zero_rows, scale_rows)
        return jnp.dot(grad_float, weight.astype(jnp.float32).T, precision=lax.Precision.HIGHEST)

    parts = lax.map(one_block, jnp.arange(INPUT_CHANNELS // block, dtype=jnp.int32))
    quantized_gradient = jnp.transpose(parts, (1, 0, 2)).reshape(TOKENS, INPUT_CHANNELS)
    adapter_inner_total = jnp.dot(output_gradient, adapter_up_matrix.T, preferred_element_type=jnp.float32)
    adapter_gradient = jnp.dot(adapter_inner_total, adapter_down_matrix.astype(jnp.float32).T, precision=lax.Precision.HIGHEST)
    return (quantized_gradient / channel_aware_scale[None, :] + adapter_gain * adapter_gradient).astype(jnp.bfloat16)
```

```python
import jax
import jax.numpy as jnp
from jax import lax
from jax.experimental import pallas as pl
from jax.experimental.pallas import tpu as pltpu
from jax.sharding import PartitionSpec as P

GROUP = 128
HALF = 128
ADAPTER_GAIN = 0.5

Z, X, YLO, YHI, CORE = 8, 4, 2, 4, 2
PLANE = X * YLO

PLANES = [[z * PLANE + p for p in range(PLANE)] for z in range(Z)]
OTHER_CORE = [(h * CORE + c, h * CORE + 1 - c) for h in range(YHI) for c in range(CORE)]


BOTH = ("wide", "narrow")


def device(z, place, h, core):
    return ((z % Z * PLANE + place) * YHI + h) * CORE + core


SPOTS = [(z, place, h) for z in range(Z) for place in range(PLANE) for h in range(YHI)]
TO_HOME = [(device(z, p, h, 1 - z % 2), device(z, p, h, z % 2)) for z, p, h in SPOTS]

OWNERS = [
    [device(z, p, ((z + (c != z % 2)) % Z // 2 + j) % YHI, c) for j in range(YHI)]
    for z in range(Z)
    for p in range(PLANE)
    for c in range(CORE)
]


def hop(step, from_home):
    cores = [(z, p, h, z % 2 if from_home else 1 - z % 2) for z, p, h in SPOTS]
    return [(device(z, p, h, c), device(z + step, p, h, c)) for z, p, h, c in cores]


def pick_row(table, index):
    rows = lax.broadcasted_iota(jnp.int32, table.shape, 0)
    return jnp.sum(jnp.where(rows == index, table, 0), axis=0, keepdims=True)


def pick_row(table, index):
    rows = lax.broadcasted_iota(jnp.int32, table.shape, 0)
    return jnp.sum(jnp.where(rows == index, table, 0), axis=0, keepdims=True)


def weight_kernel(words_ref, zero_ref, scale_ref, channel_ref, down_ref, up_ref, out_ref):
    group = pl.program_id(0)
    square = (GROUP, GROUP)
    diagonal = lax.broadcasted_iota(jnp.int32, square, 0) == lax.broadcasted_iota(jnp.int32, square, 1)
    channel = jnp.sum(jnp.where(diagonal, channel_ref[...], 0.0), axis=1, keepdims=True)
    inverse = 1.0 / channel
    down = down_ref[...]
    for block in range(words_ref.shape[1] // HALF):
        words = words_ref[:, block * HALF : (block + 1) * HALF]
        for half, codes in enumerate((words & 15, words >> 4)):
            columns = pl.ds((2 * block + half) * HALF, HALF)
            zero = pick_row(zero_ref[:, columns], group)
            scale = pick_row(scale_ref[:, columns], group)
            weight = ((codes - zero).astype(jnp.float32) * scale).astype(jnp.bfloat16)
            adapter = lax.dot_general(
                down, up_ref[:, columns], (((0,), (0,)), ((), ())), preferred_element_type=jnp.float32
            )
            out_ref[:, columns] = (
                weight.astype(jnp.float32) * inverse + ADAPTER_GAIN * adapter
            ).astype(jnp.bfloat16)


def effective_weight(words, zeros, scales, channel, down, up):
    rows, half_cols = words.shape
    cols = 2 * half_cols
    groups = rows // GROUP
    rank = down.shape[1]
    return pl.pallas_call(
        weight_kernel,
        grid=(groups,),
        in_specs=[
            pl.BlockSpec((GROUP, half_cols), lambda g: (g, 0)),
            pl.BlockSpec((groups, cols), lambda g: (0, 0)),
            pl.BlockSpec((groups, cols), lambda g: (0, 0)),
            pl.BlockSpec((1, GROUP), lambda g: (0, g)),
            pl.BlockSpec((rank, GROUP), lambda g: (0, g)),
            pl.BlockSpec((rank, cols), lambda g: (0, 0)),
        ],
        out_specs=pl.BlockSpec((GROUP, cols), lambda g: (g, 0)),
        out_shape=jax.ShapeDtypeStruct((rows, cols), jnp.bfloat16),
        compiler_params=pltpu.CompilerParams(vmem_limit_bytes=8 * 1024 * 1024),
        cost_estimate=pl.CostEstimate(
            flops=12 * rows * cols, bytes_accessed=4 * rows * half_cols + 2 * rows * cols, transcendentals=0
        ),
    )(words, zeros, scales, channel.reshape(1, rows), down.T, up)


def send_all(block, groups):
    copies = jnp.broadcast_to(block[None], (len(groups[0]),) + block.shape)
    return lax.all_to_all(copies, "wide", 0, 0, axis_index_groups=groups)


def times(block, weight, other_weight):
    dims = (((1,), (1,)), ((), ()))
    return lax.dot_general(block[0], weight, dims, preferred_element_type=jnp.float32) + lax.dot_general(
        block[1], other_weight, dims, preferred_element_type=jnp.float32
    )


def shards(grad, words, zeros, scales, channel, down, up):
    rows, cols = grad.shape
    k = words.shape[0]
    tokens = PLANE * rows
    mid = tokens // 2
    z = lax.axis_index("wide") >> 3
    core = lax.axis_index("narrow") & 1
    home = core == (z & 1)

    own = send_all(grad, PLANES).reshape(tokens, cols)
    own = jnp.stack([own, lax.ppermute(own, BOTH, TO_HOME)])

    weight = effective_weight(words, zeros, scales, channel + 0 * own[1, 0, :k].astype(jnp.float32), down, up)
    other_weight = jnp.concatenate(
        [lax.ppermute(weight[i : i + 256], "narrow", OTHER_CORE) for i in range(0, k, 256)], 0
    )
    low, high = [own], [own]
    for step in range(3):
        low.append(lax.ppermute(low[-1], BOTH, hop(1, step % 2 == 0)))
        high.append(lax.ppermute(high[-1], BOTH, hop(-1, step % 2 == 0)))
    far = jnp.concatenate(
        [
            lax.ppermute(low[3][:, :mid], BOTH, hop(1, False)),
            lax.ppermute(high[3][:, mid:], BOTH, hop(-1, False)),
        ],
        1,
    )
    blocks = [
        jnp.where(home, own, high[1]),
        jnp.where(home, high[2], high[3]),
        jnp.where(home, far, low[3]),
        jnp.where(home, low[2], low[1]),
    ]
    blocks = [lax.optimization_barrier(block) for block in blocks]
    parts = jnp.stack([times(block, weight, other_weight).astype(jnp.bfloat16) for block in blocks])
    parts = lax.all_to_all(parts, BOTH, 0, 0, axis_index_groups=OWNERS)
    return jnp.sum(parts.astype(jnp.float32), axis=0).astype(jnp.bfloat16)


def solution(mesh):
    placed = (
        P("wide", "narrow"),
        P("wide", "narrow"),
        P("wide", "narrow"),
        P("wide", "narrow"),
        P("wide"),
        P("wide", None),
        P(None, "narrow"),
    )
    return jax.shard_map(
        shards, mesh=mesh, in_specs=placed, out_specs=P("narrow", "wide"), check_vma=False
    )
```

```python
import jax
import jax.numpy as jnp
from jax import lax
from jax.experimental import pallas as pl
from jax.experimental.pallas import tpu as pltpu
from jax.sharding import PartitionSpec as P

GROUP = 128
HALF = 128
ADAPTER_GAIN = 0.5

Z, X, YLO, YHI, CORE = 8, 4, 2, 4, 2
PLANE = X * YLO

PLANES = [[z * PLANE + p for p in range(PLANE)] for z in range(Z)]
OTHER_CORE = [(h * CORE + c, h * CORE + 1 - c) for h in range(YHI) for c in range(CORE)]


BOTH = ("wide", "narrow")


def device(z, place, h, core):
    return ((z % Z * PLANE + place) * YHI + h) * CORE + core


SPOTS = [(z, place, h) for z in range(Z) for place in range(PLANE) for h in range(YHI)]
TO_HOME = [(device(z, p, h, 1 - z % 2), device(z, p, h, z % 2)) for z, p, h in SPOTS]

OWNERS = [
    [device(z, p, ((z + (c != z % 2)) % Z // 2 + j) % YHI, c) for j in range(YHI)]
    for z in range(Z)
    for p in range(PLANE)
    for c in range(CORE)
]


def hop(step, from_home):
    cores = [(z, p, h, z % 2 if from_home else 1 - z % 2) for z, p, h in SPOTS]
    return [(device(z, p, h, c), device(z + step, p, h, c)) for z, p, h, c in cores]


def pick_row(table, index):
    rows = lax.broadcasted_iota(jnp.int32, table.shape, 0)
    return jnp.sum(jnp.where(rows == index, table, 0), axis=0, keepdims=True)


def pick_row(table, index):
    rows = lax.broadcasted_iota(jnp.int32, table.shape, 0)
    return jnp.sum(jnp.where(rows == index, table, 0), axis=0, keepdims=True)


def weight_kernel(words_ref, zero_ref, scale_ref, channel_ref, down_ref, up_ref, out_ref):
    group = pl.program_id(0)
    square = (GROUP, GROUP)
    diagonal = lax.broadcasted_iota(jnp.int32, square, 0) == lax.broadcasted_iota(jnp.int32, square, 1)
    channel = jnp.sum(jnp.where(diagonal, channel_ref[...], 0.0), axis=1, keepdims=True)
    inverse = 1.0 / channel
    down = down_ref[...]
    for block in range(words_ref.shape[1] // HALF):
        words = words_ref[:, block * HALF : (block + 1) * HALF]
        for half, codes in enumerate((words & 15, words >> 4)):
            columns = pl.ds((2 * block + half) * HALF, HALF)
            zero = pick_row(zero_ref[:, columns], group)
            scale = pick_row(scale_ref[:, columns], group)
            weight = ((codes - zero).astype(jnp.float32) * scale).astype(jnp.bfloat16)
            adapter = lax.dot_general(
                down, up_ref[:, columns], (((0,), (0,)), ((), ())), preferred_element_type=jnp.float32
            )
            out_ref[:, columns] = (
                weight.astype(jnp.float32) * inverse + ADAPTER_GAIN * adapter
            ).astype(jnp.bfloat16)


def effective_weight(words, zeros, scales, channel, down, up):
    rows, half_cols = words.shape
    cols = 2 * half_cols
    groups = rows // GROUP
    rank = down.shape[1]
    return pl.pallas_call(
        weight_kernel,
        grid=(groups,),
        in_specs=[
            pl.BlockSpec((GROUP, half_cols), lambda g: (g, 0)),
            pl.BlockSpec((groups, cols), lambda g: (0, 0)),
            pl.BlockSpec((groups, cols), lambda g: (0, 0)),
            pl.BlockSpec((1, GROUP), lambda g: (0, g)),
            pl.BlockSpec((rank, GROUP), lambda g: (0, g)),
            pl.BlockSpec((rank, cols), lambda g: (0, 0)),
        ],
        out_specs=pl.BlockSpec((GROUP, cols), lambda g: (g, 0)),
        out_shape=jax.ShapeDtypeStruct((rows, cols), jnp.bfloat16),
        compiler_params=pltpu.CompilerParams(vmem_limit_bytes=8 * 1024 * 1024),
        cost_estimate=pl.CostEstimate(
            flops=12 * rows * cols, bytes_accessed=4 * rows * half_cols + 2 * rows * cols, transcendentals=0
        ),
    )(words, zeros, scales, channel.reshape(1, rows), down.T, up)


def send_all(block, groups):
    copies = jnp.broadcast_to(block[None], (len(groups[0]),) + block.shape)
    return lax.all_to_all(copies, "wide", 0, 0, axis_index_groups=groups)


def times(block, weight, other_weight):
    dims = (((1,), (1,)), ((), ()))
    return lax.dot_general(block[0], weight, dims, preferred_element_type=jnp.float32) + lax.dot_general(
        block[1], other_weight, dims, preferred_element_type=jnp.float32
    )


def shards(grad, words, zeros, scales, channel, down, up):
    rows, cols = grad.shape
    k = words.shape[0]
    tokens = PLANE * rows
    mid = tokens // 2
    z = lax.axis_index("wide") >> 3
    core = lax.axis_index("narrow") & 1
    home = core == (z & 1)

    own = send_all(grad, PLANES).reshape(tokens, cols)
    own = jnp.stack([own, lax.ppermute(own, BOTH, TO_HOME)])

    weight = effective_weight(words, zeros, scales, channel + 0 * own[1, 0, :k].astype(jnp.float32), down, up)
    other_weight = jnp.concatenate(
        [lax.ppermute(weight[i : i + 256], "narrow", OTHER_CORE) for i in range(0, k, 256)], 0
    )
    low, high = [own], [own]
    for step in range(3):
        low.append(lax.ppermute(low[-1], BOTH, hop(1, step % 2 == 0)))
        high.append(lax.ppermute(high[-1], BOTH, hop(-1, step % 2 == 0)))
    far = jnp.concatenate(
        [
            lax.ppermute(low[3][:, :mid], BOTH, hop(1, False)),
            lax.ppermute(high[3][:, mid:], BOTH, hop(-1, False)),
        ],
        1,
    )
    blocks = [
        jnp.where(home, own, high[1]),
        jnp.where(home, high[2], high[3]),
        jnp.where(home, far, low[3]),
        jnp.where(home, low[2], low[1]),
    ]
    blocks[1:3] = [lax.optimization_barrier(block) for block in blocks[1:3]]
    pair = jnp.concatenate([blocks[0], blocks[3]], 1)
    pair = times(pair, weight, other_weight).astype(jnp.bfloat16)
    middle = [times(block, weight, other_weight).astype(jnp.bfloat16) for block in blocks[1:3]]
    parts = jnp.stack([pair[:tokens], *middle, pair[tokens:]])
    parts = lax.all_to_all(parts, BOTH, 0, 0, axis_index_groups=OWNERS)
    return jnp.sum(parts.astype(jnp.float32), axis=0).astype(jnp.bfloat16)


def solution(mesh):
    placed = (
        P("wide", "narrow"),
        P("wide", "narrow"),
        P("wide", "narrow"),
        P("wide", "narrow"),
        P("wide"),
        P("wide", None),
        P(None, "narrow"),
    )
    return jax.shard_map(
        shards, mesh=mesh, in_specs=placed, out_specs=P("narrow", "wide"), check_vma=False
    )
```

```python
import jax
import jax.numpy as jnp
from jax import lax
from jax.experimental import pallas as pl
from jax.experimental.pallas import tpu as pltpu
from jax.sharding import PartitionSpec as P

GROUP = 128
HALF = 128
CHUNK = 2
ADAPTER_GAIN = 0.5

Z, X, YLO, YHI, CORE = 8, 4, 2, 4, 2
PLANE = X * YLO

PLANES = [[z * PLANE + p for p in range(PLANE)] for z in range(Z)]
OTHER_CORE = [(h * CORE + c, h * CORE + 1 - c) for h in range(YHI) for c in range(CORE)]


BOTH = ("wide", "narrow")


def device(z, place, h, core):
    return ((z % Z * PLANE + place) * YHI + h) * CORE + core


SPOTS = [(z, place, h) for z in range(Z) for place in range(PLANE) for h in range(YHI)]
TO_HOME = [(device(z, p, h, 1 - z % 2), device(z, p, h, z % 2)) for z, p, h in SPOTS]

OWNERS = [
    [device(z, p, ((z + (c != z % 2)) % Z // 2 + j) % YHI, c) for j in range(YHI)]
    for z in range(Z)
    for p in range(PLANE)
    for c in range(CORE)
]


def hop(step, from_home):
    cores = [(z, p, h, z % 2 if from_home else 1 - z % 2) for z, p, h in SPOTS]
    return [(device(z, p, h, c), device(z + step, p, h, c)) for z, p, h, c in cores]


def pick_row(table, index):
    rows = lax.broadcasted_iota(jnp.int32, table.shape, 0)
    return jnp.sum(jnp.where(rows == index, table, 0), axis=0, keepdims=True)


def pick_row(table, index):
    rows = lax.broadcasted_iota(jnp.int32, table.shape, 0)
    return jnp.sum(jnp.where(rows == index, table, 0), axis=0, keepdims=True)


def weight_kernel(words_ref, zero_ref, scale_ref, channel_ref, down_ref, up_ref, out_ref, *chunk_refs):
    group = pl.program_id(0)
    square = (GROUP, GROUP)
    diagonal = lax.broadcasted_iota(jnp.int32, square, 0) == lax.broadcasted_iota(jnp.int32, square, 1)
    channel = jnp.sum(jnp.where(diagonal, channel_ref[...], 0.0), axis=1, keepdims=True)
    inverse = 1.0 / channel
    down = down_ref[...]
    for block in range(words_ref.shape[1] // HALF):
        words = words_ref[:, block * HALF : (block + 1) * HALF]
        for half, codes in enumerate((words & 15, words >> 4)):
            columns = pl.ds((2 * block + half) * HALF, HALF)
            zero = pick_row(zero_ref[:, columns], group)
            scale = pick_row(scale_ref[:, columns], group)
            weight = ((codes - zero).astype(jnp.float32) * scale).astype(jnp.bfloat16)
            adapter = lax.dot_general(
                down, up_ref[:, columns], (((0,), (0,)), ((), ())), preferred_element_type=jnp.float32
            )
            out_ref[:, columns] = (
                weight.astype(jnp.float32) * inverse + ADAPTER_GAIN * adapter
            ).astype(jnp.bfloat16)
    for index, chunk_ref in enumerate(chunk_refs):

        @pl.when(group // CHUNK == index)
        def _(chunk_ref=chunk_ref):
            chunk_ref[...] = out_ref[...]


def effective_weight(words, zeros, scales, channel, down, up):
    rows, half_cols = words.shape
    cols = 2 * half_cols
    groups = rows // GROUP
    rank = down.shape[1]
    return pl.pallas_call(
        weight_kernel,
        grid=(groups,),
        in_specs=[
            pl.BlockSpec((GROUP, half_cols), lambda g: (g, 0)),
            pl.BlockSpec((groups, cols), lambda g: (0, 0)),
            pl.BlockSpec((groups, cols), lambda g: (0, 0)),
            pl.BlockSpec((1, GROUP), lambda g: (0, g)),
            pl.BlockSpec((rank, GROUP), lambda g: (0, g)),
            pl.BlockSpec((rank, cols), lambda g: (0, 0)),
        ],
        out_specs=[pl.BlockSpec((GROUP, cols), lambda g: (g, 0))]
        + [
            pl.BlockSpec((GROUP, cols), lambda g, i=i: (jnp.clip(g - CHUNK * i, 0, CHUNK - 1), 0))
            for i in range(groups // CHUNK)
        ],
        out_shape=[jax.ShapeDtypeStruct((rows, cols), jnp.bfloat16)]
        + [jax.ShapeDtypeStruct((CHUNK * GROUP, cols), jnp.bfloat16)] * (groups // CHUNK),
        compiler_params=pltpu.CompilerParams(vmem_limit_bytes=12 * 1024 * 1024),
        cost_estimate=pl.CostEstimate(
            flops=12 * rows * cols, bytes_accessed=4 * rows * half_cols + 2 * rows * cols, transcendentals=0
        ),
    )(words, zeros, scales, channel.reshape(1, rows), down.T, up)


def send_all(block, groups):
    copies = jnp.broadcast_to(block[None], (len(groups[0]),) + block.shape)
    return lax.all_to_all(copies, "wide", 0, 0, axis_index_groups=groups)


def times(block, weight, other_weight):
    dims = (((1,), (1,)), ((), ()))
    return lax.dot_general(block[0], weight, dims, preferred_element_type=jnp.float32) + lax.dot_general(
        block[1], other_weight, dims, preferred_element_type=jnp.float32
    )


def shards(grad, words, zeros, scales, channel, down, up):
    rows, cols = grad.shape
    k = words.shape[0]
    tokens = PLANE * rows
    mid = tokens // 2
    z = lax.axis_index("wide") >> 3
    core = lax.axis_index("narrow") & 1
    home = core == (z & 1)

    own = send_all(grad, PLANES).reshape(tokens, cols)
    own = jnp.stack([own, lax.ppermute(own, BOTH, TO_HOME)])

    weight, *chunks = effective_weight(words, zeros, scales, channel + 0 * own[1, 0, :k].astype(jnp.float32), down, up)
    other_weight = jnp.concatenate(
        [lax.ppermute(chunk, "narrow", OTHER_CORE) for chunk in chunks], 0
    )
    low, high = [own], [own]
    for step in range(3):
        low.append(lax.ppermute(low[-1], BOTH, hop(1, step % 2 == 0)))
        high.append(lax.ppermute(high[-1], BOTH, hop(-1, step % 2 == 0)))
    far = jnp.concatenate(
        [
            lax.ppermute(low[3][:, :mid], BOTH, hop(1, False)),
            lax.ppermute(high[3][:, mid:], BOTH, hop(-1, False)),
        ],
        1,
    )
    blocks = [
        jnp.where(home, own, high[1]),
        jnp.where(home, high[2], high[3]),
        jnp.where(home, far, low[3]),
        jnp.where(home, low[2], low[1]),
    ]
    blocks[1:3] = [lax.optimization_barrier(block) for block in blocks[1:3]]
    pair = jnp.concatenate([blocks[0], blocks[3]], 1)
    pair = times(pair, weight, other_weight).astype(jnp.bfloat16)
    middle = [times(block, weight, other_weight).astype(jnp.bfloat16) for block in blocks[1:3]]
    parts = jnp.stack([pair[:tokens], *middle, pair[tokens:]])
    parts = lax.all_to_all(parts, BOTH, 0, 0, axis_index_groups=OWNERS)
    return jnp.sum(parts.astype(jnp.float32), axis=0).astype(jnp.bfloat16)


def solution(mesh):
    placed = (
        P("wide", "narrow"),
        P("wide", "narrow"),
        P("wide", "narrow"),
        P("wide", "narrow"),
        P("wide"),
        P("wide", None),
        P(None, "narrow"),
    )
    return jax.shard_map(
        shards, mesh=mesh, in_specs=placed, out_specs=P("narrow", "wide"), check_vma=False
    )
```

```python
import jax
import jax.numpy as jnp
from jax import lax
from jax.experimental import pallas as pl
from jax.experimental.pallas import tpu as pltpu
from jax.sharding import PartitionSpec as P

GROUP = 128
HALF = 128
CHUNK = 2
ADAPTER_GAIN = 0.5

Z, X, YLO, YHI, CORE = 8, 4, 2, 4, 2
PLANE = X * YLO

PLANES = [[z * PLANE + p for p in range(PLANE)] for z in range(Z)]
OTHER_CORE = [(h * CORE + c, h * CORE + 1 - c) for h in range(YHI) for c in range(CORE)]


BOTH = ("wide", "narrow")


def device(z, place, h, core):
    return ((z % Z * PLANE + place) * YHI + h) * CORE + core


SPOTS = [(z, place, h) for z in range(Z) for place in range(PLANE) for h in range(YHI)]
TO_HOME = [(device(z, p, h, 1 - z % 2), device(z, p, h, z % 2)) for z, p, h in SPOTS]

OWNERS = [
    [device(z, p, ((z + (c != z % 2)) % Z // 2 + j) % YHI, c) for j in range(YHI)]
    for z in range(Z)
    for p in range(PLANE)
    for c in range(CORE)
]


def hop(step, from_home):
    cores = [(z, p, h, z % 2 if from_home else 1 - z % 2) for z, p, h in SPOTS]
    return [(device(z, p, h, c), device(z + step, p, h, c)) for z, p, h, c in cores]


def pick_row(table, index):
    rows = lax.broadcasted_iota(jnp.int32, table.shape, 0)
    return jnp.sum(jnp.where(rows == index, table, 0), axis=0, keepdims=True)


def pick_row(table, index):
    rows = lax.broadcasted_iota(jnp.int32, table.shape, 0)
    return jnp.sum(jnp.where(rows == index, table, 0), axis=0, keepdims=True)


def weight_kernel(words_ref, zero_ref, scale_ref, channel_ref, down_ref, up_ref, out_ref, *chunk_refs):
    group = pl.program_id(0)
    square = (GROUP, GROUP)
    diagonal = lax.broadcasted_iota(jnp.int32, square, 0) == lax.broadcasted_iota(jnp.int32, square, 1)
    channel = jnp.sum(jnp.where(diagonal, channel_ref[...], 0.0), axis=1, keepdims=True)
    inverse = 1.0 / channel
    down = down_ref[...]
    for block in range(words_ref.shape[1] // HALF):
        words = words_ref[:, block * HALF : (block + 1) * HALF]
        for half, codes in enumerate((words & 15, words >> 4)):
            columns = pl.ds((2 * block + half) * HALF, HALF)
            zero = pick_row(zero_ref[:, columns], group)
            scale = pick_row(scale_ref[:, columns], group)
            weight = ((codes - zero).astype(jnp.float32) * scale).astype(jnp.bfloat16)
            adapter = lax.dot_general(
                down, up_ref[:, columns], (((0,), (0,)), ((), ())), preferred_element_type=jnp.float32
            )
            out_ref[:, columns] = (
                weight.astype(jnp.float32) * inverse + ADAPTER_GAIN * adapter
            ).astype(jnp.bfloat16)
    for index, chunk_ref in enumerate(chunk_refs):

        @pl.when(group // CHUNK == index)
        def _(chunk_ref=chunk_ref):
            chunk_ref[...] = out_ref[...]


def effective_weight(words, zeros, scales, channel, down, up):
    rows, half_cols = words.shape
    cols = 2 * half_cols
    groups = rows // GROUP
    rank = down.shape[1]
    return pl.pallas_call(
        weight_kernel,
        grid=(groups,),
        in_specs=[
            pl.BlockSpec((GROUP, half_cols), lambda g: (g, 0)),
            pl.BlockSpec((groups, cols), lambda g: (0, 0)),
            pl.BlockSpec((groups, cols), lambda g: (0, 0)),
            pl.BlockSpec((1, GROUP), lambda g: (0, g)),
            pl.BlockSpec((rank, GROUP), lambda g: (0, g)),
            pl.BlockSpec((rank, cols), lambda g: (0, 0)),
        ],
        out_specs=[pl.BlockSpec((GROUP, cols), lambda g: (g, 0))]
        + [
            pl.BlockSpec((GROUP, cols), lambda g, i=i: (jnp.clip(g - CHUNK * i, 0, CHUNK - 1), 0))
            for i in range(groups // CHUNK)
        ],
        out_shape=[jax.ShapeDtypeStruct((rows, cols), jnp.bfloat16)]
        + [jax.ShapeDtypeStruct((CHUNK * GROUP, cols), jnp.bfloat16)] * (groups // CHUNK),
        compiler_params=pltpu.CompilerParams(vmem_limit_bytes=12 * 1024 * 1024),
        cost_estimate=pl.CostEstimate(
            flops=12 * rows * cols, bytes_accessed=4 * rows * half_cols + 2 * rows * cols, transcendentals=0
        ),
    )(words, zeros, scales, channel.reshape(1, rows), down.T, up)


def send_all(block, groups):
    copies = jnp.broadcast_to(block[None], (len(groups[0]),) + block.shape)
    return lax.all_to_all(copies, "wide", 0, 0, axis_index_groups=groups)


def times(block, weight, other_weight):
    dims = (((1,), (1,)), ((), ()))
    return lax.dot_general(block[0], weight, dims, preferred_element_type=jnp.float32) + lax.dot_general(
        block[1], other_weight, dims, preferred_element_type=jnp.float32
    )


def shards(grad, words, zeros, scales, channel, down, up):
    rows, cols = grad.shape
    k = words.shape[0]
    tokens = PLANE * rows
    mid = tokens // 2
    z = lax.axis_index("wide") >> 3
    core = lax.axis_index("narrow") & 1
    home = core == (z & 1)

    own = send_all(grad, PLANES).reshape(tokens, cols)
    own = jnp.stack([own, lax.ppermute(own, BOTH, TO_HOME)])

    weight, *chunks = effective_weight(words, zeros, scales, channel + 0 * own[1, 0, :k].astype(jnp.float32), down, up)
    other_weight = jnp.concatenate(
        [lax.ppermute(chunk, "narrow", OTHER_CORE) for chunk in chunks], 0
    )
    low, high = [own], [own]
    for step in range(3):
        low.append(lax.ppermute(low[-1], BOTH, hop(1, step % 2 == 0)))
        high.append(lax.ppermute(high[-1], BOTH, hop(-1, step % 2 == 0)))
    far = jnp.concatenate(
        [
            lax.ppermute(low[3][:, :mid], BOTH, hop(1, False)),
            lax.ppermute(high[3][:, mid:], BOTH, hop(-1, False)),
        ],
        1,
    )
    blocks = [
        jnp.where(home, own, high[1]),
        jnp.where(home, high[2], high[3]),
        jnp.where(home, far, low[3]),
        jnp.where(home, low[2], low[1]),
    ]
    early, late = [
        times(jnp.concatenate([blocks[i], blocks[j]], 1), weight, other_weight).astype(jnp.bfloat16)
        for i, j in ((0, 3), (1, 2))
    ]
    parts = jnp.stack([early[:tokens], late[:tokens], late[tokens:], early[tokens:]])
    parts = lax.all_to_all(parts, BOTH, 0, 0, axis_index_groups=OWNERS)
    return jnp.sum(parts.astype(jnp.float32), axis=0).astype(jnp.bfloat16)


def solution(mesh):
    placed = (
        P("wide", "narrow"),
        P("wide", "narrow"),
        P("wide", "narrow"),
        P("wide", "narrow"),
        P("wide"),
        P("wide", None),
        P(None, "narrow"),
    )
    return jax.shard_map(
        shards, mesh=mesh, in_specs=placed, out_specs=P("narrow", "wide"), check_vma=False
    )
```
